32 devices in a mesh: rep: 2 (over x), fsdp: 4 (over z), ctx: 4 (over y, core).
Axes of the slice: x: 2, y: 2, z: 4, core: 2. Of those that a mesh axis runs over, the one named last changes fastest.
Arguments:
- tokens: bfloat16 [8, 1024, 768], P(('rep', 'fsdp'), 'ctx'), may hold values from -6 to 6
- norm_one_gain: bfloat16 [1, 768], P(None, ('fsdp', 'ctx')), may hold values from 0.5 to 1.5
- norm_one_bias: bfloat16 [1, 768], P(None, ('fsdp', 'ctx')), may hold values from -3 to 3
- query_key_value: bfloat16 [1, 768, 2304], P(None, ('fsdp', 'ctx')), may hold values from -0.21875 to 0.21875
- query_value_bias: bfloat16 [1, 1536], P(None, ('fsdp', 'ctx')), may hold values from -3 to 3
- attention_out: bfloat16 [1, 768, 768], P(None, ('fsdp', 'ctx')), may hold values from -0.875 to 0.875
- attention_bias: bfloat16 [1, 768], P(None, ('fsdp', 'ctx')), may hold values from -3 to 3
- norm_two_gain: bfloat16 [1, 768], P(None, ('fsdp', 'ctx')), may hold values from 0.5 to 1.5
- norm_two_bias: bfloat16 [1, 768], P(None, ('fsdp', 'ctx')), may hold values from -3 to 3
- expand_weight: bfloat16 [1, 768, 3072], P(None, ('fsdp', 'ctx')), may hold values from -0.21875 to 0.21875
- expand_bias: bfloat16 [1, 3072], P(None, ('fsdp', 'ctx')), may hold values from -3 to 3
- contract_weight: bfloat16 [1, 3072, 768], P(None, ('fsdp', 'ctx')), may hold values from -0.109375 to 0.109375
- contract_bias: bfloat16 [1, 768], P(None, ('fsdp', 'ctx')), may hold values from -3 to 3
- cotangent: bfloat16 [8, 1024, 768], P(('rep', 'fsdp'), 'ctx'), may hold values from -6 to 6
Outputs:
- block_output: bfloat16 [8, 1024, 768], P(('rep', 'fsdp'), 'ctx')
- tokens_gradient: float32 [8, 1024, 768], P(('rep', 'fsdp'), 'ctx')
- norm_one_gain_gradient: float32 [1, 768], P(None, ('fsdp', 'ctx'))
- norm_one_bias_gradient: float32 [1, 768], P(None, ('fsdp', 'ctx'))
- query_key_value_gradient: float32 [1, 768, 2304], P(None, ('fsdp', 'ctx'))
- query_value_bias_gradient: float32 [1, 1536], P(None, ('fsdp', 'ctx'))
- attention_out_gradient: float32 [1, 768, 768], P(None, ('fsdp', 'ctx'))
- attention_bias_gradient: float32 [1, 768], P(None, ('fsdp', 'ctx'))
- norm_two_gain_gradient: float32 [1, 768], P(None, ('fsdp', 'ctx'))
- norm_two_bias_gradient: float32 [1, 768], P(None, ('fsdp', 'ctx'))
- expand_weight_gradient: float32 [1, 768, 3072], P(None, ('fsdp', 'ctx'))
- expand_bias_gradient: float32 [1, 3072], P(None, ('fsdp', 'ctx'))
- contract_weight_gradient: float32 [1, 3072, 768], P(None, ('fsdp', 'ctx'))
- contract_bias_gradient: float32 [1, 768], P(None, ('fsdp', 'ctx'))
The draws below stay inside these ranges and needn't reach their ends.
All inputs are finite; a program needn't handle non-finite values.
Results may differ from the reference program's by a relative error of at most 0.018.
Values may be sent and summed in bfloat16 or wider, within the bound.
A program may use at most 128 MiB of HBM per device.

```python
import math
import jax
import jax.numpy as jnp
from jax import lax

D = 768
H = 12
HD = 64
FF = 3072
LEN = 1024
LAYERS = 1
SEQS = 8


def level_of(key, extent, pieces, low, high):
    loudness = 1.0
    for dim, parts in pieces:
        heights = jax.random.uniform(jax.random.fold_in(jax.random.fold_in(key, 6), dim), (parts,), jnp.float32, low / len(pieces), high / len(pieces))
        loudness = loudness * jnp.repeat(jnp.exp(heights), extent[dim] // parts).reshape((-1,) + (1,) * (len(extent) - 1 - dim))
    return loudness


def bell_draw(rng, shape, scale, reach, cuts=(), dtype=jnp.bfloat16):
    loudness = level_of(rng, shape, cuts, -0.22, 0.18) if cuts else 1.0
    values = jax.random.normal(rng, shape, jnp.float32) * scale * loudness
    return jnp.minimum(jnp.maximum(values, -reach), reach).astype(dtype)


def setup_inputs(seed: int = 0) -> dict:
    keys = jax.random.split(jax.random.key(seed), 15)
    tokens = bell_draw(keys[0], (SEQS, LEN, D), 1.0, 6.0, ((0, 8), (1, 4)))
    norm_one_gain = jnp.clip(1.0 + 0.1 * jax.random.normal(keys[1], (LAYERS, D), jnp.float32), 0.5, 1.5).astype(jnp.bfloat16)
    norm_one_bias = bell_draw(keys[2], (LAYERS, D), 0.5, 3.0, ((1, 16),))
    query_key_value = bell_draw(keys[3], (LAYERS, D, 3 * D), D ** -0.5, 0.21875, ((1, 16),))
    query_value_bias = bell_draw(keys[4], (LAYERS, 2 * D), 0.5, 3.0, ((1, 16),))
    attention_out = bell_draw(keys[5], (LAYERS, D, D), (D // 16) ** -0.5, 0.875, ((1, 16),))
    attention_bias = bell_draw(keys[6], (LAYERS, D), 0.5, 3.0, ((1, 16),))
    norm_two_gain = jnp.clip(1.0 + 0.1 * jax.random.normal(keys[7], (LAYERS, D), jnp.float32), 0.5, 1.5).astype(jnp.bfloat16)
    norm_two_bias = bell_draw(keys[8], (LAYERS, D), 0.5, 3.0, ((1, 16),))
    expand_weight = bell_draw(keys[9], (LAYERS, D, FF), D ** -0.5, 0.21875, ((1, 16),))
    expand_bias = bell_draw(keys[10], (LAYERS, FF), 0.5, 3.0, ((1, 16),))
    contract_weight = bell_draw(keys[11], (LAYERS, FF, D), FF ** -0.5, 0.109375, ((1, 16),))
    contract_bias = bell_draw(keys[12], (LAYERS, D), 0.5, 3.0, ((1, 16),))
    cotangent = bell_draw(keys[13], (SEQS, LEN, D), 1.0, 6.0, ((0, 8), (1, 4)))
    return dict(tokens=tokens, norm_one_gain=norm_one_gain, norm_one_bias=norm_one_bias, query_key_value=query_key_value, query_value_bias=query_value_bias, attention_out=attention_out, attention_bias=attention_bias, norm_two_gain=norm_two_gain, norm_two_bias=norm_two_bias, expand_weight=expand_weight, expand_bias=expand_bias, contract_weight=contract_weight, contract_bias=contract_bias, cotangent=cotangent)


@jax.custom_vjp
def low(v):
    return lax.optimization_barrier(v.astype(jnp.bfloat16)).astype(jnp.float32)

@jax.custom_vjp
def low_back(v):
    return v

def low_keep(v):
    return (low(v), None)

def low_pass(kept, grad):
    return (grad,)

def back_keep(v):
    return (v, None)

def back_low(kept, grad):
    return (low(grad),)
low.defvjp(low_keep, low_pass)
low_back.defvjp(back_keep, back_low)

def norm_apply(values, gain_row, shift_row):
    center = values - lax.optimization_barrier(jnp.mean(values, axis=-1, keepdims=True))
    spread = lax.optimization_barrier(jnp.mean(center * center, axis=-1, keepdims=True))
    return center * lax.rsqrt(spread + 1e-05) * gain_row + shift_row

def matmul(left, right):
    return jnp.dot(left, right, precision=lax.Precision.HIGHEST, preferred_element_type=jnp.float32)

def attend(sequence_item):
    queries, key_rows, value_rows = sequence_item
    factor = 1.0 / math.sqrt(HD)
    scores = low_back(jnp.einsum('qhd,khd->hqk', queries, key_rows, precision=lax.Precision.HIGHEST) * factor)
    places = jnp.arange(LEN)
    allowed = places[None, :] <= places[:, None]
    scores = jnp.where(allowed[None], scores, -1e+30)
    soft_weights = jax.nn.softmax(scores, axis=-1)
    return jnp.einsum('hqk,khd->qhd', low(soft_weights), value_rows, precision=lax.Precision.HIGHEST)

def block_layer(params, hidden, sequences):
    g_one, s_one, w_joint, b_joint, w_attend, b_attend, g_two, s_two, w_expand, b_expand, w_contract, b_contract = params
    normed_one = low(norm_apply(hidden, g_one, s_one))
    bias_row = jnp.concatenate([b_joint[:D], jnp.zeros((D,), jnp.float32), b_joint[D:]])
    joint_rows = low(low_back(matmul(normed_one, w_joint) + bias_row))
    shaped = joint_rows.reshape(sequences, LEN, 3, H, HD)
    mixture = lax.map(jax.checkpoint(attend), (shaped[:, :, 0], shaped[:, :, 1], shaped[:, :, 2]))
    mixture = low(low_back(mixture.reshape(-1, D)))
    after_attend = hidden + low_back(matmul(mixture, w_attend) + b_attend)
    normed_two = low(norm_apply(after_attend, g_two, s_two))
    expanded = low_back(matmul(normed_two, w_expand) + b_expand)
    activated = low(jax.nn.gelu(expanded, approximate=True))
    return after_attend + low_back(matmul(activated, w_contract) + b_contract)

def forward(params, hidden_block):
    sequences = hidden_block.shape[0]
    hidden = hidden_block.reshape(-1, D)
    for layer_at in range(LAYERS):
        hidden = block_layer(tuple((stacked[layer_at] for stacked in params)), hidden, sequences)
    return hidden.reshape(hidden_block.shape)

def reference(tokens, norm_one_gain, norm_one_bias, query_key_value, query_value_bias, attention_out, attention_bias, norm_two_gain, norm_two_bias, expand_weight, expand_bias, contract_weight, contract_bias, cotangent):
    params = tuple((stacked.astype(jnp.float32) for stacked in (norm_one_gain, norm_one_bias, query_key_value, query_value_bias, attention_out, attention_bias, norm_two_gain, norm_two_bias, expand_weight, expand_bias, contract_weight, contract_bias)))
    per_block = math.gcd(SEQS, max(1, 4096 // LEN))
    blocks = SEQS // per_block
    inputs = tokens.astype(jnp.float32).reshape(blocks, per_block, LEN, D)
    upstream = cotangent.astype(jnp.float32).reshape(blocks, per_block, LEN, D)

    def advance(totals, pair_item):
        block_in, block_up = pair_item
        result, backward = jax.vjp(forward, params, block_in)
        param_grads, input_grad = backward(block_up)
        return (jax.tree.map(jnp.add, totals, param_grads), (result, input_grad))
    zeros_init = tuple((jnp.zeros_like(stacked) for stacked in params))
    totals, (results, input_grads) = lax.scan(advance, zeros_init, (inputs, upstream))
    return (results.reshape(SEQS, LEN, D).astype(jnp.bfloat16), input_grads.reshape(SEQS, LEN, D), totals[0], totals[1], totals[2], totals[3], totals[4], totals[5], totals[6], totals[7], totals[8], totals[9], totals[10], totals[11])
```

```python
import functools
import math

import jax
import jax.numpy as jnp
from jax import lax
from jax.experimental import pallas as pl
from jax.experimental.pallas import tpu as pltpu
from jax.sharding import PartitionSpec as P

H = 12
F32 = jnp.float32
BF16 = jnp.bfloat16
MASKED = -1e30
ROWS = 256


def dot(left, right, contract):
    return lax.dot_general(
        left, right, (((contract[0],), (contract[1],)), ((), ())), preferred_element_type=F32
    )


def norm_apply(values, gain_row, shift_row):
    center = values - jnp.mean(values, axis=-1, keepdims=True)
    spread = jnp.mean(center * center, axis=-1, keepdims=True)
    return center * lax.rsqrt(spread + 1e-05) * gain_row + shift_row


def norm_back(values, gain_row, upstream):
    center = values - jnp.mean(values, axis=-1, keepdims=True)
    scale = lax.rsqrt(jnp.mean(center * center, axis=-1, keepdims=True) + 1e-05)
    unit = center * scale
    e = upstream * gain_row
    grad = scale * (
        e - jnp.mean(e, axis=-1, keepdims=True) - unit * jnp.mean(e * unit, axis=-1, keepdims=True)
    )
    return grad, jnp.sum(upstream * unit, axis=0), jnp.sum(upstream, axis=0)


def causal(first_row, rows, keys):
    row = first_row + lax.broadcasted_iota(jnp.int32, (rows, keys), 0)
    key = lax.broadcasted_iota(jnp.int32, (rows, keys), 1)
    return key <= row


def attend_fwd(head, x, gain, shift, bias, w_joint, w_out, normed, joint, mix, logsum, part):
    length = x.shape[0]
    width = w_out.shape[0]
    heads = width // head
    factor = 1.0 / math.sqrt(head)
    for first in range(0, length, ROWS):
        rows = pl.ds(first, ROWS)
        last = first + ROWS
        h1 = norm_apply(x[rows, :].astype(F32), gain[...], shift[...]).astype(BF16)
        normed[rows, :] = h1
        joint[rows, :] = (dot(h1, w_joint[...], (1, 0)) + bias[...]).astype(BF16)
        allowed = causal(first, ROWS, last)
        outs = []
        for h in range(heads):
            q = joint[rows, pl.ds(h * head, head)]
            k = joint[pl.ds(0, last), pl.ds(width + h * head, head)]
            v = joint[pl.ds(0, last), pl.ds(2 * width + h * head, head)]
            s = jnp.where(allowed, dot(q, k, (1, 1)) * factor, MASKED)
            top = jnp.max(s, axis=-1, keepdims=True)
            p = jnp.exp(s - top)
            total = jnp.sum(p, axis=-1, keepdims=True)
            outs.append(dot((p * (1.0 / total)).astype(BF16), v, (1, 0)))
            logsum[rows, pl.ds(h, 1)] = top + jnp.log(total)
        o = jnp.concatenate(outs, axis=1).astype(BF16)
        mix[rows, :] = o
        part[rows, :] = dot(o, w_out[...], (1, 0)).astype(BF16)


def feed_both(h2, dm, w_up, b_up, w_down, part, dh2, d_up, d_down, d_bias, act, du):
    length = h2.shape[0]
    c0 = math.sqrt(2.0 / math.pi)
    d_bias[...] = jnp.zeros_like(d_bias)

    @pl.loop(0, length // ROWS)
    def _(at):
        rows = pl.ds(pl.multiple_of(at * ROWS, ROWS), ROWS)
        u = dot(h2[rows, :], w_up[...], (1, 0)) + b_up[...]
        square = u * u
        t = jnp.tanh(c0 * (u + 0.044715 * (u * square)))
        act[rows, :] = (0.5 * u * (1.0 + t)).astype(BF16)
        slope = 0.5 * (1.0 + t) + (0.5 * c0) * u * (1.0 - t * t) * (1.0 + (3 * 0.044715) * square)
        part[rows, :] = dot(act[rows, :], w_down[...], (1, 0)).astype(BF16)
        low = (dot(dm[rows, :], w_down[...], (1, 1)) * slope).astype(BF16)
        du[rows, :] = low
        d_bias[...] += jnp.sum(low.astype(F32), axis=0, keepdims=True)
        dh2[rows, :] = dot(low, w_up[...], (1, 1)).astype(BF16)

    d_up[...] = dot(h2[...], du[...], (0, 0)).astype(BF16)
    d_down[...] = dot(act[...], dm[...], (0, 0)).astype(BF16)


def attend_bwd(
    head, da, w_out, mix, joint, logsum, normed, w_joint, d_out, d_joint_w, sums, dh1, up, acc, low
):
    length = da.shape[0]
    width = w_out.shape[0]
    heads = width // head
    factor = 1.0 / math.sqrt(head)
    up[...] = dot(da[...], w_out[...], (1, 1)).astype(BF16)
    d_out[...] = dot(mix[...], da[...], (0, 0)).astype(BF16)
    for first in reversed(range(0, length, ROWS)):
        rows = pl.ds(first, ROWS)
        last = first + ROWS
        seen = pl.ds(0, last)
        allowed = causal(first, ROWS, last)
        for h in range(heads):
            qc = pl.ds(h * head, head)
            kc = pl.ds(width + h * head, head)
            vc = pl.ds(2 * width + h * head, head)
            q = joint[rows, qc]
            k = joint[seen, kc]
            v = joint[seen, vc]
            do = up[rows, qc]
            s = jnp.where(allowed, dot(q, k, (1, 1)) * factor, MASKED)
            p = jnp.exp(s - logsum[rows, pl.ds(h, 1)])
            dp = dot(do, v, (1, 1))
            center = jnp.sum(p * dp, axis=-1, keepdims=True)
            ds = (p * (dp - center)).astype(BF16)
            acc[rows, qc] = dot(ds, k, (1, 0)) * factor
            dk = dot(ds, q, (0, 0)) * factor
            dv = dot(p.astype(BF16), do, (0, 0))
            if last == length:
                acc[seen, kc] = dk
                acc[seen, vc] = dv
            else:
                acc[seen, kc] += dk
                acc[seen, vc] += dv
    low[...] = acc[...].astype(BF16)
    sums[...] = jnp.sum(low[...].astype(F32), axis=0, keepdims=True)
    d_joint_w[...] = dot(normed[...], low[...], (0, 0)).astype(BF16)
    for first in range(0, length, ROWS):
        rows = pl.ds(first, ROWS)
        dh1[rows, :] = dot(low[rows, :], w_joint[...], (1, 1)).astype(BF16)


def local_call(body, outs, scratch, flops, nbytes, args):
    return pl.pallas_call(
        body,
        out_shape=tuple(jax.ShapeDtypeStruct(shape, kind) for shape, kind in outs),
        in_specs=[pl.BlockSpec(memory_space=pltpu.VMEM)] * len(args),
        out_specs=tuple(pl.BlockSpec(memory_space=pltpu.VMEM) for _ in outs),
        scratch_shapes=[pltpu.VMEM(shape, kind) for shape, kind in scratch],
        compiler_params=pltpu.CompilerParams(vmem_limit_bytes=48 * 1024 * 1024),
        cost_estimate=pl.CostEstimate(flops=flops, bytes_accessed=nbytes, transcendentals=0),
    )(*args)


def swap_sum(value, replicas):
    low = value.astype(BF16)
    if replicas == 1:
        return low.astype(F32)
    if replicas == 2:
        other = lax.ppermute(low, "rep", [(0, 1), (1, 0)])
        return low.astype(F32) + other.astype(F32)
    return lax.psum(low, "rep").astype(F32)


def on_device(sizes, *args):
    replicas, nf, nc = sizes
    (
        tokens,
        g_one,
        s_one,
        w_joint,
        b_joint,
        w_attend,
        b_attend,
        g_two,
        s_two,
        w_expand,
        b_expand,
        w_contract,
        b_contract,
        cotangent,
    ) = args
    _, per_seq, d = tokens.shape
    length = per_seq * nc
    own = w_joint.shape[1]
    head = d // H
    width = d // nc
    part_ff = w_contract.shape[1]
    ff = part_ff * nf
    turn = [(f * nc + c, c * nc + f) for f in range(nf) for c in range(nc)]
    at_f, at_c = lax.axis_index("fsdp"), lax.axis_index("ctx")

    x_low = tokens[0]
    x_all = lax.all_gather(x_low, "ctx", axis=0, tiled=True)
    vec = jnp.concatenate(
        [v[0] for v in (g_one, s_one, b_attend, g_two, s_two, b_contract, b_joint, b_expand)]
    )
    count = vec.shape[0]
    pad = -own % 64
    block = w_joint[0].reshape(own, 3, nc, width).transpose(2, 0, 1, 3).reshape(nc, own, 3 * width)
    vec_rows = jnp.pad(vec.reshape(1, count), ((0, pad - 1), (0, 3 * width - count)))
    block = jnp.concatenate([block, jnp.broadcast_to(vec_rows[None], (nc, pad, 3 * width))], axis=1)
    block = lax.all_to_all(block, "ctx", 0, 0, tiled=True)
    block = lax.all_gather(block, "fsdp", axis=0, tiled=True)
    wj = block[:, :own].reshape(d, 3 * width)
    vecs = block[:, own, :count].astype(F32)
    g1, s1, ba, g2, s2, bc = (vecs[:, n * own : (n + 1) * own].reshape(1, d) for n in range(6))
    bj = vecs[:, 6 * own : 8 * own].reshape(2, nc, width)
    bj = lax.dynamic_index_in_dim(bj, at_c, 1, keepdims=False)
    bj = jnp.concatenate([bj[0], jnp.zeros((width,), F32), bj[1]]).reshape(1, 3 * width)
    be = vecs[:, 8 * own :].reshape(nf, nc, part_ff)
    be = lax.dynamic_index_in_dim(be, at_c, 1, keepdims=False).reshape(1, ff)

    wo = lax.ppermute(w_attend[0], ("fsdp", "ctx"), turn)
    wo = lax.all_gather(wo, "fsdp", axis=0, tiled=True)
    we = w_expand[0].reshape(own, nf, nc, part_ff).transpose(2, 0, 1, 3).reshape(nc, own, ff)
    we = lax.all_to_all(we, "ctx", 0, 0, tiled=True).reshape(nc * own, ff)
    we = lax.all_gather(we, "fsdp", axis=0, tiled=True)
    wc = lax.all_gather(w_contract[0], "fsdp", axis=0, tiled=True)
    dm_all = lax.all_gather(cotangent[0], "ctx", axis=0, tiled=True)

    normed, joint, mix, logsum, part = local_call(
        functools.partial(attend_fwd, head),
        (
            ((length, d), BF16),
            ((length, 3 * width), BF16),
            ((length, width), BF16),
            ((length, 128), F32),
            ((length, d), BF16),
        ),
        (),
        2 * length * d * 4 * width + 4 * length * length * width,
        12 * length * d,
        (x_all, g1, s1, bj, wj, wo),
    )
    x = x_low.astype(F32)
    mixed = lax.psum_scatter(part, "ctx", scatter_dimension=0, tiled=True).astype(F32)
    x1 = x + (mixed + ba)
    h2 = norm_apply(x1, g2, s2).astype(BF16)
    h2_all = lax.all_gather(h2, "ctx", axis=0, tiled=True)

    down, dh2, d_up, d_down, d_be = local_call(
        feed_both,
        (
            ((length, d), BF16),
            ((length, d), BF16),
            ((d, ff), BF16),
            ((ff, d), BF16),
            ((1, ff), F32),
        ),
        (((length, ff), BF16), ((length, ff), BF16)),
        12 * length * d * ff,
        18 * length * d,
        (h2_all, dm_all, we, be, wc),
    )
    dh2 = lax.psum_scatter(dh2, "ctx", scatter_dimension=0, tiled=True).astype(F32)
    dx = cotangent[0].astype(F32)
    back, d_g2, d_s2 = norm_back(x1, g2, dh2)
    dx1 = dx + back
    da = dx1.astype(BF16)
    da_all = lax.all_gather(da, "ctx", axis=0, tiled=True)
    down = lax.psum_scatter(down, "ctx", scatter_dimension=0, tiled=True).astype(F32)
    block_out = (x1 + (down + bc)).astype(BF16)

    d_wo, d_wj, sums, dh1 = local_call(
        functools.partial(attend_bwd, head),
        (
            ((width, d), BF16),
            ((d, 3 * width), BF16),
            ((1, 3 * width), F32),
            ((length, d), BF16),
        ),
        (
            ((length, width), BF16),
            ((length, 3 * width), F32),
            ((length, 3 * width), BF16),
        ),
        4 * length * d * 4 * width + 10 * length * length * width,
        12 * length * d,
        (da_all, wo, mix, joint, logsum, normed, wj),
    )
    dh1 = lax.psum_scatter(dh1, "ctx", scatter_dimension=0, tiled=True).astype(F32)
    back, d_g1, d_s1 = norm_back(x, g1, dh1)
    grad_tokens = dx1 + back

    out_wc = lax.psum_scatter(d_down, "fsdp", scatter_dimension=0, tiled=True)
    out_wc = swap_sum(out_wc, replicas)
    out_we = lax.psum_scatter(d_up, "fsdp", scatter_dimension=0, tiled=True)
    out_we = lax.all_to_all(out_we.reshape(nc, own, ff), "ctx", 0, 0, tiled=True)
    out_we = out_we.reshape(nc, own, nf, part_ff).transpose(1, 2, 0, 3).reshape(own, nf * nc * part_ff)
    out_we = swap_sum(out_we, replicas)
    out_wo = lax.psum_scatter(d_wo, "fsdp", scatter_dimension=0, tiled=True)
    out_wo = lax.ppermute(out_wo, ("fsdp", "ctx"), [(b, a) for a, b in turn])
    out_wo = swap_sum(out_wo, replicas)

    d_ba = jnp.sum(da.astype(F32), axis=0)
    d_bc = jnp.sum(dx, axis=0)
    mine = (jnp.arange(nc) == at_c).astype(F32)
    sums = sums.reshape(3, 1, width)
    d_bj = jnp.stack([sums[0], sums[2]]) * mine[None, :, None]
    d_be = d_be.reshape(nf, 1, part_ff) * mine[None, :, None]
    groups = nf * nc
    d_vec = jnp.concatenate(
        [v.reshape(groups, own) for v in (d_g1, d_s1, d_ba, d_g2, d_s2, d_bc)]
        + [d_bj.reshape(groups, 2 * own), d_be.reshape(groups, part_ff)],
        axis=1,
    ).astype(BF16)
    d_vec = jnp.pad(d_vec.reshape(groups, 1, count), ((0, 0), (0, pad - 1), (0, 3 * width - count)))
    tail = jnp.concatenate([d_wj.reshape(groups, own, 3 * width), d_vec], axis=1)
    tail = lax.psum_scatter(tail, "fsdp", scatter_dimension=0, tiled=True)
    tail = lax.all_to_all(tail, "ctx", 0, 0, tiled=True)
    out_vec = jnp.sum(tail[:, own, :count].astype(F32), axis=0)
    out_wj = tail[:, :own].reshape(nc, own, 3, width).transpose(1, 2, 0, 3).reshape(own, 3 * d)
    out_vec = swap_sum(out_vec.reshape(1, count), replicas)
    out_wj = swap_sum(out_wj, replicas)

    v = [out_vec[:, n * own : (n + 1) * own] for n in range(6)]
    return (
        block_out[None],
        grad_tokens[None],
        v[0],
        v[1],
        out_wj[None],
        out_vec[:, 6 * own : 8 * own],
        out_wo[None],
        v[2],
        v[3],
        v[4],
        out_we[None],
        out_vec[:, 8 * own :],
        out_wc[None],
        v[5],
    )


def solution(mesh):
    rows = P(("rep", "fsdp"), "ctx", None)
    vector = P(None, ("fsdp", "ctx"))
    matrix = P(None, ("fsdp", "ctx"), None)
    params = (
        vector,
        vector,
        matrix,
        vector,
        matrix,
        vector,
        vector,
        vector,
        matrix,
        vector,
        matrix,
        vector,
    )
    sizes = (mesh.shape["rep"], mesh.shape["fsdp"], mesh.shape["ctx"])
    return jax.shard_map(
        functools.partial(on_device, sizes),
        mesh=mesh,
        in_specs=(rows,) + params + (rows,),
        out_specs=(rows, rows) + params,
        check_vma=False,
    )
```

```python
import functools
import math

import jax
import jax.numpy as jnp
from jax import lax
from jax.experimental import pallas as pl
from jax.experimental.pallas import tpu as pltpu
from jax.sharding import PartitionSpec as P

H = 12
F32 = jnp.float32
BF16 = jnp.bfloat16
MASKED = -1e30
ROWS = 256


def dot(left, right, contract):
    return lax.dot_general(
        left, right, (((contract[0],), (contract[1],)), ((), ())), preferred_element_type=F32
    )


def norm_apply(values, gain_row, shift_row):
    center = values - jnp.mean(values, axis=-1, keepdims=True)
    spread = jnp.mean(center * center, axis=-1, keepdims=True)
    return center * lax.rsqrt(spread + 1e-05) * gain_row + shift_row


def norm_back(values, gain_row, upstream):
    center = values - jnp.mean(values, axis=-1, keepdims=True)
    scale = lax.rsqrt(jnp.mean(center * center, axis=-1, keepdims=True) + 1e-05)
    unit = center * scale
    e = upstream * gain_row
    grad = scale * (
        e - jnp.mean(e, axis=-1, keepdims=True) - unit * jnp.mean(e * unit, axis=-1, keepdims=True)
    )
    return grad, jnp.sum(upstream * unit, axis=0), jnp.sum(upstream, axis=0)


def causal(first_row, rows, keys):
    row = first_row + lax.broadcasted_iota(jnp.int32, (rows, keys), 0)
    key = lax.broadcasted_iota(jnp.int32, (rows, keys), 1)
    return key <= row


def attend_fwd(head, x, gain, shift, bias, w_joint, w_out, normed, joint, mix, logsum, part):
    length = x.shape[0]
    width = w_out.shape[0]
    heads = width // head
    factor = 1.0 / math.sqrt(head)
    for first in range(0, length, ROWS):
        rows = pl.ds(first, ROWS)
        last = first + ROWS
        h1 = norm_apply(x[rows, :].astype(F32), gain[...], shift[...]).astype(BF16)
        normed[rows, :] = h1
        joint[rows, :] = (dot(h1, w_joint[...], (1, 0)) + bias[...]).astype(BF16)
        allowed = causal(first, ROWS, last)
        outs = []
        for h in range(heads):
            q = joint[rows, pl.ds(h * head, head)]
            k = joint[pl.ds(0, last), pl.ds(width + h * head, head)]
            v = joint[pl.ds(0, last), pl.ds(2 * width + h * head, head)]
            s = jnp.where(allowed, dot(q, k, (1, 1)) * factor, MASKED)
            top = jnp.max(s, axis=-1, keepdims=True)
            p = jnp.exp(s - top)
            total = jnp.sum(p, axis=-1, keepdims=True)
            outs.append(dot((p * (1.0 / total)).astype(BF16), v, (1, 0)))
            logsum[rows, pl.ds(h, 1)] = top + jnp.log(total)
        o = jnp.concatenate(outs, axis=1).astype(BF16)
        mix[rows, :] = o
        part[rows, :] = dot(o, w_out[...], (1, 0)).astype(BF16)


def feed_both(h2, dm, w_up, b_up, w_down, part, dh2, d_up, d_down, d_bias, act, du):
    length = h2.shape[0]
    c0 = math.sqrt(2.0 / math.pi)
    d_bias[...] = jnp.zeros_like(d_bias)

    @pl.loop(0, length // ROWS)
    def _(at):
        rows = pl.ds(pl.multiple_of(at * ROWS, ROWS), ROWS)
        u = dot(h2[rows, :], w_up[...], (1, 0)) + b_up[...]
        square = u * u
        t = jnp.tanh(c0 * (u + 0.044715 * (u * square)))
        act[rows, :] = (0.5 * u * (1.0 + t)).astype(BF16)
        slope = 0.5 * (1.0 + t) + (0.5 * c0) * u * (1.0 - t * t) * (1.0 + (3 * 0.044715) * square)
        part[rows, :] = dot(act[rows, :], w_down[...], (1, 0)).astype(BF16)
        low = (dot(dm[rows, :], w_down[...], (1, 1)) * slope).astype(BF16)
        du[rows, :] = low
        d_bias[...] += jnp.sum(low.astype(F32), axis=0, keepdims=True)
        dh2[rows, :] = dot(low, w_up[...], (1, 1)).astype(BF16)

    d_up[...] = dot(h2[...], du[...], (0, 0)).astype(BF16)
    d_down[...] = dot(act[...], dm[...], (0, 0)).astype(BF16)


def attend_bwd(
    head, da, w_out, mix, joint, logsum, normed, w_joint, d_out, d_joint_w, sums, dh1, up, acc, low
):
    length = da.shape[0]
    width = w_out.shape[0]
    heads = width // head
    factor = 1.0 / math.sqrt(head)
    up[...] = dot(da[...], w_out[...], (1, 1)).astype(BF16)
    d_out[...] = dot(mix[...], da[...], (0, 0)).astype(BF16)
    for first in reversed(range(0, length, ROWS)):
        rows = pl.ds(first, ROWS)
        last = first + ROWS
        seen = pl.ds(0, last)
        allowed = causal(first, ROWS, last)
        for h in range(heads):
            qc = pl.ds(h * head, head)
            kc = pl.ds(width + h * head, head)
            vc = pl.ds(2 * width + h * head, head)
            q = joint[rows, qc]
            k = joint[seen, kc]
            v = joint[seen, vc]
            do = up[rows, qc]
            s = jnp.where(allowed, dot(q, k, (1, 1)) * factor, MASKED)
            p = jnp.exp(s - logsum[rows, pl.ds(h, 1)])
            dp = dot(do, v, (1, 1))
            center = jnp.sum(p * dp, axis=-1, keepdims=True)
            ds = (p * (dp - center)).astype(BF16)
            acc[rows, qc] = dot(ds, k, (1, 0)) * factor
            dk = dot(ds, q, (0, 0)) * factor
            dv = dot(p.astype(BF16), do, (0, 0))
            if last == length:
                acc[seen, kc] = dk
                acc[seen, vc] = dv
            else:
                acc[seen, kc] += dk
                acc[seen, vc] += dv
    low[...] = acc[...].astype(BF16)
    sums[...] = jnp.sum(low[...].astype(F32), axis=0, keepdims=True)
    d_joint_w[...] = dot(normed[...], low[...], (0, 0)).astype(BF16)
    for first in range(0, length, ROWS):
        rows = pl.ds(first, ROWS)
        dh1[rows, :] = dot(low[rows, :], w_joint[...], (1, 1)).astype(BF16)


def local_call(body, outs, scratch, flops, nbytes, args):
    return pl.pallas_call(
        body,
        out_shape=tuple(jax.ShapeDtypeStruct(shape, kind) for shape, kind in outs),
        in_specs=[pl.BlockSpec(memory_space=pltpu.VMEM)] * len(args),
        out_specs=tuple(pl.BlockSpec(memory_space=pltpu.VMEM) for _ in outs),
        scratch_shapes=[pltpu.VMEM(shape, kind) for shape, kind in scratch],
        compiler_params=pltpu.CompilerParams(vmem_limit_bytes=48 * 1024 * 1024),
        cost_estimate=pl.CostEstimate(flops=flops, bytes_accessed=nbytes, transcendentals=0),
    )(*args)


CHUNKS = 4


class Ctx:
    def __init__(self, send_sem, recv_sem):
        self.me = lax.axis_index("ctx")
        high, low = self.me // 2, self.me % 2
        self.sibling = high * 2 + (1 - low)
        self.across = (1 - high) * 2 + low
        self.diagonal = (1 - high) * 2 + (1 - low)
        self.send_sem, self.recv_sem = send_sem, recv_sem
        self.sent = []

    def enter(self):
        barrier = pltpu.get_barrier_semaphore()
        for partner in (self.sibling, self.across):
            pl.semaphore_signal(
                barrier,
                inc=1,
                device_id={"ctx": partner},
                device_id_type=pl.DeviceIdType.MESH,
            )
        pl.semaphore_wait(barrier, 2)

    def send(self, src, dst, slot, partner):
        copy = pltpu.make_async_remote_copy(
            src_ref=src,
            dst_ref=dst,
            send_sem=self.send_sem.at[slot],
            recv_sem=self.recv_sem.at[slot],
            device_id={"ctx": partner},
            device_id_type=pl.DeviceIdType.MESH,
        )
        copy.start()
        self.sent.append(copy)
        return copy

    def leave(self):
        for copy in self.sent:
            copy.wait_send()


def block_rows(block, rows, chunk):
    size = rows // CHUNKS
    return pl.ds(pl.multiple_of(block * rows + chunk * size, size), size)


def gather_send(ctx, whole, rows, chunk, slot):
    at = block_rows(ctx.me, rows, chunk)
    return (
        ctx.send(whole.at[at], whole.at[at], slot + 1, ctx.across),
        ctx.send(whole.at[at], whole.at[at], slot, ctx.sibling),
    )


def gather_finish(ctx, whole, rows, copies, slot):
    passed = []
    for chunk in range(CHUNKS):
        copies[chunk][0].wait_recv()
        at = block_rows(ctx.across, rows, chunk)
        passed.append(ctx.send(whole.at[at], whole.at[at], slot + 3 * chunk + 2, ctx.sibling))
    for chunk in range(CHUNKS):
        copies[chunk][1].wait_recv()
        passed[chunk].wait_recv()


def scatter_start(ctx, part, near, rows, slot):
    copies = []
    size = rows // CHUNKS
    for side, block in enumerate((ctx.diagonal, ctx.sibling)):
        for chunk in range(CHUNKS):
            copies.append(
                ctx.send(
                    part.at[block_rows(block, rows, chunk)],
                    near.at[side, pl.ds(chunk * size, size)],
                    slot + side * CHUNKS + chunk,
                    ctx.sibling,
                )
            )
    return copies


def scatter_across(ctx, part, near, out, far, rows, copies, slot):
    size = rows // CHUNKS
    for chunk in range(CHUNKS):
        copies[chunk].wait_recv()
        here = pl.ds(chunk * size, size)
        out[here, :] = (
            part[block_rows(ctx.across, rows, chunk), :].astype(F32) + near[0, here, :].astype(F32)
        ).astype(BF16)
        copies.append(
            ctx.send(out.at[here], far.at[here], slot + 2 * CHUNKS + chunk, ctx.across)
        )


def scatter_take(ctx, part, near, far, rows, copies, chunk):
    size = rows // CHUNKS
    here = pl.ds(chunk * size, size)
    copies[CHUNKS + chunk].wait_recv()
    copies[2 * CHUNKS + chunk].wait_recv()
    own = part[block_rows(ctx.me, rows, chunk), :].astype(F32)
    return own + near[1, here, :].astype(F32) + far[here, :].astype(F32)


def gather_inputs(x, up, x_all, up_all, send_sem, recv_sem):
    ctx = Ctx(send_sem, recv_sem)
    ctx.enter()
    rows = x.shape[0]
    size = rows // CHUNKS
    kept = []
    for index, (own, whole) in enumerate(((x, x_all), (up, up_all))):
        copies = []
        for chunk in range(CHUNKS):
            whole[block_rows(ctx.me, rows, chunk), :] = own[pl.ds(chunk * size, size), :]
            copies.append(gather_send(ctx, whole, rows, chunk, 3 * CHUNKS * index + 3 * chunk))
        kept.append(copies)
    for index, whole in enumerate((x_all, up_all)):
        gather_finish(ctx, whole, rows, kept[index], 3 * CHUNKS * index)
    ctx.leave()


def between_forward(
    part, x, bias, gain, shift, x1, whole, near, out, far, send_sem, recv_sem
):
    ctx = Ctx(send_sem, recv_sem)
    ctx.enter()
    rows = x.shape[0]
    size = rows // CHUNKS
    arrived = scatter_start(ctx, part, near, rows, 0)
    scatter_across(ctx, part, near, out, far, rows, arrived, 0)
    copies = []
    for chunk in range(CHUNKS):
        here = pl.ds(chunk * size, size)
        total = scatter_take(ctx, part, near, far, rows, arrived, chunk)
        value = x[here, :].astype(F32) + (total + bias[...])
        x1[here, :] = value
        whole[block_rows(ctx.me, rows, chunk), :] = norm_apply(
            value, gain[...], shift[...]
        ).astype(BF16)
        copies.append(gather_send(ctx, whole, rows, chunk, 3 * CHUNKS + 3 * chunk))
    gather_finish(ctx, whole, rows, copies, 3 * CHUNKS)
    ctx.leave()


def between_backward(
    part, x1, up, gain, dx1, whole, d_gain, d_shift, d_bias, near, out, far, send_sem, recv_sem
):
    ctx = Ctx(send_sem, recv_sem)
    ctx.enter()
    rows = x1.shape[0]
    size = rows // CHUNKS
    arrived = scatter_start(ctx, part, near, rows, 0)
    for total in (d_gain, d_shift, d_bias):
        total[...] = jnp.zeros_like(total)
    scatter_across(ctx, part, near, out, far, rows, arrived, 0)
    copies = []
    for chunk in range(CHUNKS):
        here = pl.ds(chunk * size, size)
        total = scatter_take(ctx, part, near, far, rows, arrived, chunk)
        back, gain_part, shift_part = norm_back(x1[here, :], gain[...], total)
        value = up[here, :].astype(F32) + back
        dx1[here, :] = value
        low = value.astype(BF16)
        whole[block_rows(ctx.me, rows, chunk), :] = low
        copies.append(gather_send(ctx, whole, rows, chunk, 3 * CHUNKS + 3 * chunk))
        d_gain[...] += gain_part[None]
        d_shift[...] += shift_part[None]
        d_bias[...] += jnp.sum(low.astype(F32), axis=0, keepdims=True)
    gather_finish(ctx, whole, rows, copies, 3 * CHUNKS)
    ctx.leave()


def sum_block(down, x1, bias, block, near, out, far, send_sem, recv_sem):
    ctx = Ctx(send_sem, recv_sem)
    ctx.enter()
    rows = x1.shape[0]
    size = rows // CHUNKS
    arrived = scatter_start(ctx, down, near, rows, 0)
    scatter_across(ctx, down, near, out, far, rows, arrived, 0)
    for chunk in range(CHUNKS):
        here = pl.ds(chunk * size, size)
        total = scatter_take(ctx, down, near, far, rows, arrived, chunk)
        block[here, :] = (x1[here, :] + (total + bias[...])).astype(BF16)
    ctx.leave()


def sum_grad(grad, x, gain, dx1, dx, d_gain, d_shift, near, out, far, send_sem, recv_sem):
    ctx = Ctx(send_sem, recv_sem)
    ctx.enter()
    rows = x.shape[0]
    size = rows // CHUNKS
    arrived = scatter_start(ctx, grad, near, rows, 0)
    for total in (d_gain, d_shift):
        total[...] = jnp.zeros_like(total)
    scatter_across(ctx, grad, near, out, far, rows, arrived, 0)
    for chunk in range(CHUNKS):
        here = pl.ds(chunk * size, size)
        total = scatter_take(ctx, grad, near, far, rows, arrived, chunk)
        back, gain_part, shift_part = norm_back(x[here, :].astype(F32), gain[...], total)
        dx[here, :] = dx1[here, :] + back
        d_gain[...] += gain_part[None]
        d_shift[...] += shift_part[None]
    ctx.leave()


def linked_call(body, number, outs, scratch, slots, args):
    return pl.pallas_call(
        body,
        out_shape=tuple(jax.ShapeDtypeStruct(shape, kind) for shape, kind in outs),
        in_specs=[pl.BlockSpec(memory_space=pltpu.VMEM)] * len(args),
        out_specs=tuple(pl.BlockSpec(memory_space=pltpu.VMEM) for _ in outs),
        scratch_shapes=[pltpu.VMEM(shape, kind) for shape, kind in scratch]
        + [pltpu.SemaphoreType.DMA((slots,)), pltpu.SemaphoreType.DMA((slots,))],
        compiler_params=pltpu.CompilerParams(
            collective_id=number, has_side_effects=True, vmem_limit_bytes=32 * 1024 * 1024
        ),
        cost_estimate=pl.CostEstimate(
            flops=10_000_000_000, bytes_accessed=40_000_000, transcendentals=0
        ),
    )(*args)


def swap_sum(value, replicas):
    low = value.astype(BF16)
    if replicas == 1:
        return low.astype(F32)
    if replicas == 2:
        other = lax.ppermute(low, "rep", [(0, 1), (1, 0)])
        return low.astype(F32) + other.astype(F32)
    return lax.psum(low, "rep").astype(F32)


def on_device(sizes, *args):
    replicas, nf, nc = sizes
    (
        tokens,
        g_one,
        s_one,
        w_joint,
        b_joint,
        w_attend,
        b_attend,
        g_two,
        s_two,
        w_expand,
        b_expand,
        w_contract,
        b_contract,
        cotangent,
    ) = args
    _, per_seq, d = tokens.shape
    length = per_seq * nc
    own = w_joint.shape[1]
    head = d // H
    width = d // nc
    part_ff = w_contract.shape[1]
    ff = part_ff * nf
    turn = [(f * nc + c, c * nc + f) for f in range(nf) for c in range(nc)]
    at_f, at_c = lax.axis_index("fsdp"), lax.axis_index("ctx")

    x_low = tokens[0]
    exchange = (((2, per_seq, d), BF16), ((per_seq, d), BF16), ((per_seq, d), BF16))
    whole = ((length, d), BF16)
    x_all, dm_all = linked_call(
        gather_inputs, 0, (whole, whole), (), 6 * CHUNKS, (x_low, cotangent[0])
    )
    vec = jnp.concatenate(
        [v[0] for v in (g_one, s_one, b_attend, g_two, s_two, b_contract, b_joint, b_expand)]
    )
    count = vec.shape[0]
    pad = -own % 64
    block = w_joint[0].reshape(own, 3, nc, width).transpose(2, 0, 1, 3).reshape(nc, own, 3 * width)
    vec_rows = jnp.pad(vec.reshape(1, count), ((0, pad - 1), (0, 3 * width - count)))
    block = jnp.concatenate([block, jnp.broadcast_to(vec_rows[None], (nc, pad, 3 * width))], axis=1)
    block = lax.all_to_all(block, "ctx", 0, 0, tiled=True)
    block = lax.all_gather(block, "fsdp", axis=0, tiled=True)
    wj = block[:, :own].reshape(d, 3 * width)
    vecs = block[:, own, :count].astype(F32)
    g1, s1, ba, g2, s2, bc = (vecs[:, n * own : (n + 1) * own].reshape(1, d) for n in range(6))
    bj = vecs[:, 6 * own : 8 * own].reshape(2, nc, width)
    bj = lax.dynamic_index_in_dim(bj, at_c, 1, keepdims=False)
    bj = jnp.concatenate([bj[0], jnp.zeros((width,), F32), bj[1]]).reshape(1, 3 * width)
    be = vecs[:, 8 * own :].reshape(nf, nc, part_ff)
    be = lax.dynamic_index_in_dim(be, at_c, 1, keepdims=False).reshape(1, ff)

    wo = lax.ppermute(w_attend[0], ("fsdp", "ctx"), turn)
    wo = lax.all_gather(wo, "fsdp", axis=0, tiled=True)
    we = w_expand[0].reshape(own, nf, nc, part_ff).transpose(2, 0, 1, 3).reshape(nc, own, ff)
    we = lax.all_to_all(we, "ctx", 0, 0, tiled=True).reshape(nc * own, ff)
    we = lax.all_gather(we, "fsdp", axis=0, tiled=True)
    wc = lax.all_gather(w_contract[0], "fsdp", axis=0, tiled=True)

    normed, joint, mix, logsum, part = local_call(
        functools.partial(attend_fwd, head),
        (
            ((length, d), BF16),
            ((length, 3 * width), BF16),
            ((length, width), BF16),
            ((length, 128), F32),
            ((length, d), BF16),
        ),
        (),
        2 * length * d * 4 * width + 4 * length * length * width,
        12 * length * d,
        (x_all, g1, s1, bj, wj, wo),
    )
    x1, h2_all = linked_call(
        between_forward,
        1,
        (((per_seq, d), F32), whole),
        exchange,
        6 * CHUNKS,
        (part, x_low, ba, g2, s2),
    )

    down, dh2, d_up, d_down, d_be = local_call(
        feed_both,
        (
            ((length, d), BF16),
            ((length, d), BF16),
            ((d, ff), BF16),
            ((ff, d), BF16),
            ((1, ff), F32),
        ),
        (((length, ff), BF16), ((length, ff), BF16)),
        12 * length * d * ff,
        18 * length * d,
        (h2_all, dm_all, we, be, wc),
    )
    row = ((1, d), F32)
    dx1, da_all, d_g2, d_s2, d_ba = linked_call(
        between_backward,
        2,
        (((per_seq, d), F32), whole, row, row, row),
        exchange,
        6 * CHUNKS,
        (dh2, x1, cotangent[0], g2),
    )

    d_wo, d_wj, sums, dh1 = local_call(
        functools.partial(attend_bwd, head),
        (
            ((width, d), BF16),
            ((d, 3 * width), BF16),
            ((1, 3 * width), F32),
            ((length, d), BF16),
        ),
        (
            ((length, width), BF16),
            ((length, 3 * width), F32),
            ((length, 3 * width), BF16),
        ),
        4 * length * d * 4 * width + 10 * length * length * width,
        12 * length * d,
        (da_all, wo, mix, joint, logsum, normed, wj),
    )
    (block_out,) = linked_call(
        sum_block, 3, (((per_seq, d), BF16),), exchange, 3 * CHUNKS, (down, x1, bc)
    )
    out_wc = lax.psum_scatter(d_down, "fsdp", scatter_dimension=0, tiled=True)
    out_we = lax.psum_scatter(d_up, "fsdp", scatter_dimension=0, tiled=True)
    dh1, block_out, out_wc, out_we = lax.optimization_barrier((dh1, block_out, out_wc, out_we))
    grad_tokens, d_g1, d_s1 = linked_call(
        sum_grad,
        4,
        (((per_seq, d), F32), row, row),
        exchange,
        3 * CHUNKS,
        (dh1, x_low, g1, dx1),
    )

    out_wc = swap_sum(out_wc, replicas)
    out_we = lax.all_to_all(out_we.reshape(nc, own, ff), "ctx", 0, 0, tiled=True)
    out_we = out_we.reshape(nc, own, nf, part_ff).transpose(1, 2, 0, 3).reshape(own, nf * nc * part_ff)
    out_we = swap_sum(out_we, replicas)
    out_wo = lax.psum_scatter(d_wo, "fsdp", scatter_dimension=0, tiled=True)
    out_wo = lax.ppermute(out_wo, ("fsdp", "ctx"), [(b, a) for a, b in turn])
    out_wo = swap_sum(out_wo, replicas)

    d_bc = jnp.sum(cotangent[0].astype(F32), axis=0)
    mine = (jnp.arange(nc) == at_c).astype(F32)
    sums = sums.reshape(3, 1, width)
    d_bj = jnp.stack([sums[0], sums[2]]) * mine[None, :, None]
    d_be = d_be.reshape(nf, 1, part_ff) * mine[None, :, None]
    groups = nf * nc
    d_vec = jnp.concatenate(
        [v.reshape(groups, own) for v in (d_g1, d_s1, d_ba, d_g2, d_s2, d_bc)]
        + [d_bj.reshape(groups, 2 * own), d_be.reshape(groups, part_ff)],
        axis=1,
    ).astype(BF16)
    d_vec = jnp.pad(d_vec.reshape(groups, 1, count), ((0, 0), (0, pad - 1), (0, 3 * width - count)))
    tail = jnp.concatenate([d_wj.reshape(groups, own, 3 * width), d_vec], axis=1)
    tail = lax.psum_scatter(tail, "fsdp", scatter_dimension=0, tiled=True)
    tail = lax.all_to_all(tail, "ctx", 0, 0, tiled=True)
    out_vec = jnp.sum(tail[:, own, :count].astype(F32), axis=0)
    out_wj = tail[:, :own].reshape(nc, own, 3, width).transpose(1, 2, 0, 3).reshape(own, 3 * d)
    out_vec = swap_sum(out_vec.reshape(1, count), replicas)
    out_wj = swap_sum(out_wj, replicas)

    v = [out_vec[:, n * own : (n + 1) * own] for n in range(6)]
    return (
        block_out[None],
        grad_tokens[None],
        v[0],
        v[1],
        out_wj[None],
        out_vec[:, 6 * own : 8 * own],
        out_wo[None],
        v[2],
        v[3],
        v[4],
        out_we[None],
        out_vec[:, 8 * own :],
        out_wc[None],
        v[5],
    )


def solution(mesh):
    rows = P(("rep", "fsdp"), "ctx", None)
    vector = P(None, ("fsdp", "ctx"))
    matrix = P(None, ("fsdp", "ctx"), None)
    params = (
        vector,
        vector,
        matrix,
        vector,
        matrix,
        vector,
        vector,
        vector,
        matrix,
        vector,
        matrix,
        vector,
    )
    sizes = (mesh.shape["rep"], mesh.shape["fsdp"], mesh.shape["ctx"])
    return jax.shard_map(
        functools.partial(on_device, sizes),
        mesh=mesh,
        in_specs=(rows,) + params + (rows,),
        out_specs=(rows, rows) + params,
        check_vma=False,
    )
```

```python
import functools
import math

import jax
import jax.numpy as jnp
from jax import lax
from jax.experimental import pallas as pl
from jax.experimental.pallas import tpu as pltpu
from jax.sharding import PartitionSpec as P

H = 12
F32 = jnp.float32
BF16 = jnp.bfloat16
MASKED = -1e30
ROWS = 256


def dot(left, right, contract):
    return lax.dot_general(
        left, right, (((contract[0],), (contract[1],)), ((), ())), preferred_element_type=F32
    )


def norm_apply(values, gain_row, shift_row):
    center = values - jnp.mean(values, axis=-1, keepdims=True)
    spread = jnp.mean(center * center, axis=-1, keepdims=True)
    return center * lax.rsqrt(spread + 1e-05) * gain_row + shift_row


def norm_back(values, gain_row, upstream):
    center = values - jnp.mean(values, axis=-1, keepdims=True)
    scale = lax.rsqrt(jnp.mean(center * center, axis=-1, keepdims=True) + 1e-05)
    unit = center * scale
    e = upstream * gain_row
    grad = scale * (
        e - jnp.mean(e, axis=-1, keepdims=True) - unit * jnp.mean(e * unit, axis=-1, keepdims=True)
    )
    return grad, jnp.sum(upstream * unit, axis=0), jnp.sum(upstream, axis=0)


def causal(first_row, rows, keys):
    row = first_row + lax.broadcasted_iota(jnp.int32, (rows, keys), 0)
    key = lax.broadcasted_iota(jnp.int32, (rows, keys), 1)
    return key <= row


def attend_fwd(head, x, gain, shift, bias, w_joint, w_out, normed, joint, mix, logsum, part):
    length = x.shape[0]
    width = w_out.shape[0]
    heads = width // head
    factor = 1.0 / math.sqrt(head)
    for first in range(0, length, ROWS):
        rows = pl.ds(first, ROWS)
        last = first + ROWS
        h1 = norm_apply(x[rows, :].astype(F32), gain[...], shift[...]).astype(BF16)
        normed[rows, :] = h1
        joint[rows, :] = (dot(h1, w_joint[...], (1, 0)) + bias[...]).astype(BF16)
        allowed = causal(first, ROWS, last)
        outs = []
        for h in range(heads):
            q = joint[rows, pl.ds(h * head, head)]
            k = joint[pl.ds(0, last), pl.ds(width + h * head, head)]
            v = joint[pl.ds(0, last), pl.ds(2 * width + h * head, head)]
            s = jnp.where(allowed, dot(q, k, (1, 1)) * factor, MASKED)
            top = jnp.max(s, axis=-1, keepdims=True)
            p = jnp.exp(s - top)
            total = jnp.sum(p, axis=-1, keepdims=True)
            outs.append(dot((p * (1.0 / total)).astype(BF16), v, (1, 0)))
            logsum[rows, pl.ds(h, 1)] = top + jnp.log(total)
        o = jnp.concatenate(outs, axis=1).astype(BF16)
        mix[rows, :] = o
        part[rows, :] = dot(o, w_out[...], (1, 0)).astype(BF16)


def feed_both(h2, dm, w_up, b_up, w_down, part, dh2, d_up, d_down, d_bias, act, du):
    length = h2.shape[0]
    c0 = math.sqrt(2.0 / math.pi)
    d_bias[...] = jnp.zeros_like(d_bias)

    @pl.loop(0, length // ROWS)
    def _(at):
        rows = pl.ds(pl.multiple_of(at * ROWS, ROWS), ROWS)
        u = dot(h2[rows, :], w_up[...], (1, 0)) + b_up[...]
        square = u * u
        t = jnp.tanh(c0 * (u + 0.044715 * (u * square)))
        act[rows, :] = (0.5 * u * (1.0 + t)).astype(BF16)
        slope = 0.5 * (1.0 + t) + (0.5 * c0) * u * (1.0 - t * t) * (1.0 + (3 * 0.044715) * square)
        part[rows, :] = dot(act[rows, :], w_down[...], (1, 0)).astype(BF16)
        low = (dot(dm[rows, :], w_down[...], (1, 1)) * slope).astype(BF16)
        du[rows, :] = low
        d_bias[...] += jnp.sum(low.astype(F32), axis=0, keepdims=True)
        dh2[rows, :] = dot(low, w_up[...], (1, 1)).astype(BF16)

    d_up[...] = dot(h2[...], du[...], (0, 0)).astype(BF16)
    d_down[...] = dot(act[...], dm[...], (0, 0)).astype(BF16)


def attend_bwd(
    head, da, w_out, mix, joint, logsum, normed, w_joint, d_out, d_joint_w, sums, dh1, up, acc, low
):
    length = da.shape[0]
    width = w_out.shape[0]
    heads = width // head
    factor = 1.0 / math.sqrt(head)
    up[...] = dot(da[...], w_out[...], (1, 1)).astype(BF16)
    d_out[...] = dot(mix[...], da[...], (0, 0)).astype(BF16)
    for first in reversed(range(0, length, ROWS)):
        rows = pl.ds(first, ROWS)
        last = first + ROWS
        seen = pl.ds(0, last)
        allowed = causal(first, ROWS, last)
        for h in range(heads):
            qc = pl.ds(h * head, head)
            kc = pl.ds(width + h * head, head)
            vc = pl.ds(2 * width + h * head, head)
            q = joint[rows, qc]
            k = joint[seen, kc]
            v = joint[seen, vc]
            do = up[rows, qc]
            s = jnp.where(allowed, dot(q, k, (1, 1)) * factor, MASKED)
            p = jnp.exp(s - logsum[rows, pl.ds(h, 1)])
            dp = dot(do, v, (1, 1))
            center = jnp.sum(p * dp, axis=-1, keepdims=True)
            ds = (p * (dp - center)).astype(BF16)
            acc[rows, qc] = dot(ds, k, (1, 0)) * factor
            dk = dot(ds, q, (0, 0)) * factor
            dv = dot(p.astype(BF16), do, (0, 0))
            if last == length:
                acc[seen, kc] = dk
                acc[seen, vc] = dv
            else:
                acc[seen, kc] += dk
                acc[seen, vc] += dv
    low[...] = acc[...].astype(BF16)
    sums[...] = jnp.sum(low[...].astype(F32), axis=0, keepdims=True)
    d_joint_w[...] = dot(normed[...], low[...], (0, 0)).astype(BF16)
    for first in range(0, length, ROWS):
        rows = pl.ds(first, ROWS)
        dh1[rows, :] = dot(low[rows, :], w_joint[...], (1, 1)).astype(BF16)


def local_call(body, outs, scratch, flops, nbytes, args):
    return pl.pallas_call(
        body,
        out_shape=tuple(jax.ShapeDtypeStruct(shape, kind) for shape, kind in outs),
        in_specs=[pl.BlockSpec(memory_space=pltpu.VMEM)] * len(args),
        out_specs=tuple(pl.BlockSpec(memory_space=pltpu.VMEM) for _ in outs),
        scratch_shapes=[pltpu.VMEM(shape, kind) for shape, kind in scratch],
        compiler_params=pltpu.CompilerParams(vmem_limit_bytes=48 * 1024 * 1024),
        cost_estimate=pl.CostEstimate(flops=flops, bytes_accessed=nbytes, transcendentals=0),
    )(*args)


CHUNKS = 4


class Ctx:
    def __init__(self, send_sem, recv_sem):
        self.me = lax.axis_index("ctx")
        high, low = self.me // 2, self.me % 2
        self.sibling = high * 2 + (1 - low)
        self.across = (1 - high) * 2 + low
        self.diagonal = (1 - high) * 2 + (1 - low)
        self.send_sem, self.recv_sem = send_sem, recv_sem
        self.sent = []

    def enter(self):
        barrier = pltpu.get_barrier_semaphore()
        for partner in (self.sibling, self.across):
            pl.semaphore_signal(
                barrier,
                inc=1,
                device_id={"ctx": partner},
                device_id_type=pl.DeviceIdType.MESH,
            )
        pl.semaphore_wait(barrier, 2)

    def send(self, src, dst, slot, partner):
        copy = pltpu.make_async_remote_copy(
            src_ref=src,
            dst_ref=dst,
            send_sem=self.send_sem.at[slot],
            recv_sem=self.recv_sem.at[slot],
            device_id={"ctx": partner},
            device_id_type=pl.DeviceIdType.MESH,
        )
        copy.start()
        self.sent.append(copy)
        return copy

    def leave(self):
        for copy in self.sent:
            copy.wait_send()


def block_rows(block, rows, chunk):
    size = rows // CHUNKS
    return pl.ds(pl.multiple_of(block * rows + chunk * size, size), size)


def gather_send(ctx, whole, rows, chunk, slot):
    at = block_rows(ctx.me, rows, chunk)
    return (
        ctx.send(whole.at[at], whole.at[at], slot + 1, ctx.across),
        ctx.send(whole.at[at], whole.at[at], slot, ctx.sibling),
    )


def gather_finish(ctx, whole, rows, copies, slot):
    passed = []
    for chunk in range(CHUNKS):
        copies[chunk][0].wait_recv()
        at = block_rows(ctx.across, rows, chunk)
        passed.append(ctx.send(whole.at[at], whole.at[at], slot + 3 * chunk + 2, ctx.sibling))
    for chunk in range(CHUNKS):
        copies[chunk][1].wait_recv()
        passed[chunk].wait_recv()


def scatter_start(ctx, part, near, rows, slot):
    copies = []
    size = rows // CHUNKS
    for side, block in enumerate((ctx.diagonal, ctx.sibling)):
        for chunk in range(CHUNKS):
            copies.append(
                ctx.send(
                    part.at[block_rows(block, rows, chunk)],
                    near.at[side, pl.ds(chunk * size, size)],
                    slot + side * CHUNKS + chunk,
                    ctx.sibling,
                )
            )
    return copies


def scatter_across(ctx, part, near, out, far, rows, copies, slot):
    size = rows // CHUNKS
    for chunk in range(CHUNKS):
        copies[chunk].wait_recv()
        here = pl.ds(chunk * size, size)
        out[here, :] = (
            part[block_rows(ctx.across, rows, chunk), :].astype(F32) + near[0, here, :].astype(F32)
        ).astype(BF16)
        copies.append(
            ctx.send(out.at[here], far.at[here], slot + 2 * CHUNKS + chunk, ctx.across)
        )


def scatter_take(ctx, part, near, far, rows, copies, chunk):
    size = rows // CHUNKS
    here = pl.ds(chunk * size, size)
    copies[CHUNKS + chunk].wait_recv()
    copies[2 * CHUNKS + chunk].wait_recv()
    own = part[block_rows(ctx.me, rows, chunk), :].astype(F32)
    return own + near[1, here, :].astype(F32) + far[here, :].astype(F32)


def gather_inputs(x, up, x_all, up_all, send_sem, recv_sem):
    ctx = Ctx(send_sem, recv_sem)
    ctx.enter()
    rows = x.shape[0]
    size = rows // CHUNKS
    kept = []
    for index, (own, whole) in enumerate(((x, x_all), (up, up_all))):
        copies = []
        for chunk in range(CHUNKS):
            whole[block_rows(ctx.me, rows, chunk), :] = own[pl.ds(chunk * size, size), :]
            copies.append(gather_send(ctx, whole, rows, chunk, 3 * CHUNKS * index + 3 * chunk))
        kept.append(copies)
    for index, whole in enumerate((x_all, up_all)):
        gather_finish(ctx, whole, rows, kept[index], 3 * CHUNKS * index)
    ctx.leave()


def between_forward(
    part, x, bias, gain, shift, x1, whole, near, out, far, send_sem, recv_sem
):
    ctx = Ctx(send_sem, recv_sem)
    ctx.enter()
    rows = x.shape[0]
    size = rows // CHUNKS
    arrived = scatter_start(ctx, part, near, rows, 0)
    scatter_across(ctx, part, near, out, far, rows, arrived, 0)
    copies = []
    for chunk in range(CHUNKS):
        here = pl.ds(chunk * size, size)
        total = scatter_take(ctx, part, near, far, rows, arrived, chunk)
        value = x[here, :].astype(F32) + (total + bias[...])
        x1[here, :] = value
        whole[block_rows(ctx.me, rows, chunk), :] = norm_apply(
            value, gain[...], shift[...]
        ).astype(BF16)
        copies.append(gather_send(ctx, whole, rows, chunk, 3 * CHUNKS + 3 * chunk))
    gather_finish(ctx, whole, rows, copies, 3 * CHUNKS)
    ctx.leave()


def between_backward(
    part, x1, up, gain, dx1, whole, d_gain, d_shift, d_bias, near, out, far, send_sem, recv_sem
):
    ctx = Ctx(send_sem, recv_sem)
    ctx.enter()
    rows = x1.shape[0]
    size = rows // CHUNKS
    arrived = scatter_start(ctx, part, near, rows, 0)
    for total in (d_gain, d_shift, d_bias):
        total[...] = jnp.zeros_like(total)
    scatter_across(ctx, part, near, out, far, rows, arrived, 0)
    copies = []
    for chunk in range(CHUNKS):
        here = pl.ds(chunk * size, size)
        total = scatter_take(ctx, part, near, far, rows, arrived, chunk)
        back, gain_part, shift_part = norm_back(x1[here, :], gain[...], total)
        value = up[here, :].astype(F32) + back
        dx1[here, :] = value
        low = value.astype(BF16)
        whole[block_rows(ctx.me, rows, chunk), :] = low
        copies.append(gather_send(ctx, whole, rows, chunk, 3 * CHUNKS + 3 * chunk))
        d_gain[...] += gain_part[None]
        d_shift[...] += shift_part[None]
        d_bias[...] += jnp.sum(low.astype(F32), axis=0, keepdims=True)
    gather_finish(ctx, whole, rows, copies, 3 * CHUNKS)
    ctx.leave()


def sum_block(down, x1, bias, block, near, out, far, send_sem, recv_sem):
    ctx = Ctx(send_sem, recv_sem)
    ctx.enter()
    rows = x1.shape[0]
    size = rows // CHUNKS
    arrived = scatter_start(ctx, down, near, rows, 0)
    scatter_across(ctx, down, near, out, far, rows, arrived, 0)
    for chunk in range(CHUNKS):
        here = pl.ds(chunk * size, size)
        total = scatter_take(ctx, down, near, far, rows, arrived, chunk)
        block[here, :] = (x1[here, :] + (total + bias[...])).astype(BF16)
    ctx.leave()


def sum_grad(grad, x, gain, dx1, dx, d_gain, d_shift, near, out, far, send_sem, recv_sem):
    ctx = Ctx(send_sem, recv_sem)
    ctx.enter()
    rows = x.shape[0]
    size = rows // CHUNKS
    arrived = scatter_start(ctx, grad, near, rows, 0)
    for total in (d_gain, d_shift):
        total[...] = jnp.zeros_like(total)
    scatter_across(ctx, grad, near, out, far, rows, arrived, 0)
    for chunk in range(CHUNKS):
        here = pl.ds(chunk * size, size)
        total = scatter_take(ctx, grad, near, far, rows, arrived, chunk)
        back, gain_part, shift_part = norm_back(x[here, :].astype(F32), gain[...], total)
        dx[here, :] = dx1[here, :] + back
        d_gain[...] += gain_part[None]
        d_shift[...] += shift_part[None]
    ctx.leave()


def linked_call(body, number, outs, scratch, slots, args):
    return pl.pallas_call(
        body,
        out_shape=tuple(jax.ShapeDtypeStruct(shape, kind) for shape, kind in outs),
        in_specs=[pl.BlockSpec(memory_space=pltpu.VMEM)] * len(args),
        out_specs=tuple(pl.BlockSpec(memory_space=pltpu.VMEM) for _ in outs),
        scratch_shapes=[pltpu.VMEM(shape, kind) for shape, kind in scratch]
        + [pltpu.SemaphoreType.DMA((slots,)), pltpu.SemaphoreType.DMA((slots,))],
        compiler_params=pltpu.CompilerParams(
            collective_id=number, has_side_effects=True, vmem_limit_bytes=32 * 1024 * 1024
        ),
        cost_estimate=pl.CostEstimate(
            flops=10_000_000_000, bytes_accessed=40_000_000, transcendentals=0
        ),
    )(*args)


def swap_sum(value, replicas):
    low = value.astype(BF16)
    if replicas == 1:
        return low.astype(F32)
    if replicas == 2:
        other = lax.ppermute(low, "rep", [(0, 1), (1, 0)])
        return low.astype(F32) + other.astype(F32)
    return lax.psum(low, "rep").astype(F32)


def on_device(sizes, *args):
    replicas, nf, nc = sizes
    (
        tokens,
        g_one,
        s_one,
        w_joint,
        b_joint,
        w_attend,
        b_attend,
        g_two,
        s_two,
        w_expand,
        b_expand,
        w_contract,
        b_contract,
        cotangent,
    ) = args
    _, per_seq, d = tokens.shape
    length = per_seq * nc
    own = w_joint.shape[1]
    head = d // H
    width = d // nc
    part_ff = w_contract.shape[1]
    ff = part_ff * nf
    turn = [(f * nc + c, c * nc + f) for f in range(nf) for c in range(nc)]
    at_f, at_c = lax.axis_index("fsdp"), lax.axis_index("ctx")

    x_low = tokens[0]
    exchange = (((2, per_seq, d), BF16), ((per_seq, d), BF16), ((per_seq, d), BF16))
    whole = ((length, d), BF16)
    x_all, dm_all = linked_call(
        gather_inputs, 0, (whole, whole), (), 6 * CHUNKS, (x_low, cotangent[0])
    )
    vec = jnp.concatenate(
        [v[0] for v in (g_one, s_one, b_attend, g_two, s_two, b_contract, b_joint, b_expand)]
    )
    count = vec.shape[0]
    pad = -own % 64
    block = w_joint[0].reshape(own, 3, nc, width).transpose(2, 0, 1, 3).reshape(nc, own, 3 * width)
    vec_rows = jnp.pad(vec.reshape(1, count), ((0, pad - 1), (0, 3 * width - count)))
    block = jnp.concatenate([block, jnp.broadcast_to(vec_rows[None], (nc, pad, 3 * width))], axis=1)
    block = lax.all_to_all(block, "ctx", 0, 0, tiled=True)
    block = lax.all_gather(block, "fsdp", axis=0, tiled=True)
    wj = block[:, :own].reshape(d, 3 * width)
    vecs = block[:, own, :count].astype(F32)
    g1, s1, ba, g2, s2, bc = (vecs[:, n * own : (n + 1) * own].reshape(1, d) for n in range(6))
    bj = vecs[:, 6 * own : 8 * own].reshape(2, nc, width)
    bj = lax.dynamic_index_in_dim(bj, at_c, 1, keepdims=False)
    bj = jnp.concatenate([bj[0], jnp.zeros((width,), F32), bj[1]]).reshape(1, 3 * width)
    be = vecs[:, 8 * own :].reshape(nf, nc, part_ff)
    be = lax.dynamic_index_in_dim(be, at_c, 1, keepdims=False).reshape(1, ff)

    if nf == nc:
        pieces = [
            lax.ppermute(
                w_attend[0],
                ("fsdp", "ctx"),
                [(c * nc + (f + j) % nc, f * nc + c) for f in range(nf) for c in range(nc)],
            )
            for j in range(nc)
        ]
        wo = jnp.zeros((width, d), BF16)
        for j, piece in enumerate(pieces):
            wo = lax.dynamic_update_slice_in_dim(wo, piece, lax.rem(at_f + j, nc) * own, 0)
    else:
        wo = lax.ppermute(w_attend[0], ("fsdp", "ctx"), turn)
        wo = lax.all_gather(wo, "fsdp", axis=0, tiled=True)
    we = w_expand[0].reshape(own, nf, nc, part_ff).transpose(2, 0, 1, 3).reshape(nc, own, ff)
    we = lax.all_to_all(we, "ctx", 0, 0, tiled=True).reshape(nc * own, ff)
    we = lax.all_gather(we, "fsdp", axis=0, tiled=True)
    wc = lax.all_gather(w_contract[0], "fsdp", axis=0, tiled=True)

    normed, joint, mix, logsum, part = local_call(
        functools.partial(attend_fwd, head),
        (
            ((length, d), BF16),
            ((length, 3 * width), BF16),
            ((length, width), BF16),
            ((length, 128), F32),
            ((length, d), BF16),
        ),
        (),
        2 * length * d * 4 * width + 4 * length * length * width,
        12 * length * d,
        (x_all, g1, s1, bj, wj, wo),
    )
    x1, h2_all = linked_call(
        between_forward,
        1,
        (((per_seq, d), F32), whole),
        exchange,
        6 * CHUNKS,
        (part, x_low, ba, g2, s2),
    )

    down, dh2, d_up, d_down, d_be = local_call(
        feed_both,
        (
            ((length, d), BF16),
            ((length, d), BF16),
            ((d, ff), BF16),
            ((ff, d), BF16),
            ((1, ff), F32),
        ),
        (((length, ff), BF16), ((length, ff), BF16)),
        12 * length * d * ff,
        18 * length * d,
        (h2_all, dm_all, we, be, wc),
    )
    row = ((1, d), F32)
    dx1, da_all, d_g2, d_s2, d_ba = linked_call(
        between_backward,
        2,
        (((per_seq, d), F32), whole, row, row, row),
        exchange,
        6 * CHUNKS,
        (dh2, x1, cotangent[0], g2),
    )

    d_wo, d_wj, sums, dh1 = local_call(
        functools.partial(attend_bwd, head),
        (
            ((width, d), BF16),
            ((d, 3 * width), BF16),
            ((1, 3 * width), F32),
            ((length, d), BF16),
        ),
        (
            ((length, width), BF16),
            ((length, 3 * width), F32),
            ((length, 3 * width), BF16),
        ),
        4 * length * d * 4 * width + 10 * length * length * width,
        12 * length * d,
        (da_all, wo, mix, joint, logsum, normed, wj),
    )
    (block_out,) = linked_call(
        sum_block, 3, (((per_seq, d), BF16),), exchange, 3 * CHUNKS, (down, x1, bc)
    )
    out_wc = lax.psum_scatter(d_down, "fsdp", scatter_dimension=0, tiled=True)
    out_we = lax.psum_scatter(d_up, "fsdp", scatter_dimension=0, tiled=True)
    dh1, block_out, out_wc, out_we = lax.optimization_barrier((dh1, block_out, out_wc, out_we))
    grad_tokens, d_g1, d_s1 = linked_call(
        sum_grad,
        4,
        (((per_seq, d), F32), row, row),
        exchange,
        3 * CHUNKS,
        (dh1, x_low, g1, dx1),
    )

    out_wc = swap_sum(out_wc, replicas)
    out_we = lax.all_to_all(out_we.reshape(nc, own, ff), "ctx", 0, 0, tiled=True)
    out_we = out_we.reshape(nc, own, nf, part_ff).transpose(1, 2, 0, 3).reshape(own, nf * nc * part_ff)
    out_we = swap_sum(out_we, replicas)
    out_wo = lax.psum_scatter(d_wo, "fsdp", scatter_dimension=0, tiled=True)
    out_wo = lax.ppermute(out_wo, ("fsdp", "ctx"), [(b, a) for a, b in turn])
    out_wo = swap_sum(out_wo, replicas)

    d_bc = jnp.sum(cotangent[0].astype(F32), axis=0)
    mine = (jnp.arange(nc) == at_c).astype(F32)
    sums = sums.reshape(3, 1, width)
    d_bj = jnp.stack([sums[0], sums[2]]) * mine[None, :, None]
    d_be = d_be.reshape(nf, 1, part_ff) * mine[None, :, None]
    groups = nf * nc
    d_vec = jnp.concatenate(
        [v.reshape(groups, own) for v in (d_g1, d_s1, d_ba, d_g2, d_s2, d_bc)]
        + [d_bj.reshape(groups, 2 * own), d_be.reshape(groups, part_ff)],
        axis=1,
    ).astype(BF16)
    d_vec = jnp.pad(d_vec.reshape(groups, 1, count), ((0, 0), (0, pad - 1), (0, 3 * width - count)))
    tail = jnp.concatenate([d_wj.reshape(groups, own, 3 * width), d_vec], axis=1)
    tail = lax.psum_scatter(tail, "fsdp", scatter_dimension=0, tiled=True)
    tail = lax.all_to_all(tail, "ctx", 0, 0, tiled=True)
    out_vec = jnp.sum(tail[:, own, :count].astype(F32), axis=0)
    out_wj = tail[:, :own].reshape(nc, own, 3, width).transpose(1, 2, 0, 3).reshape(own, 3 * d)
    out_vec = swap_sum(out_vec.reshape(1, count), replicas)
    out_wj = swap_sum(out_wj, replicas)

    v = [out_vec[:, n * own : (n + 1) * own] for n in range(6)]
    return (
        block_out[None],
        grad_tokens[None],
        v[0],
        v[1],
        out_wj[None],
        out_vec[:, 6 * own : 8 * own],
        out_wo[None],
        v[2],
        v[3],
        v[4],
        out_we[None],
        out_vec[:, 8 * own :],
        out_wc[None],
        v[5],
    )


def solution(mesh):
    rows = P(("rep", "fsdp"), "ctx", None)
    vector = P(None, ("fsdp", "ctx"))
    matrix = P(None, ("fsdp", "ctx"), None)
    params = (
        vector,
        vector,
        matrix,
        vector,
        matrix,
        vector,
        vector,
        vector,
        matrix,
        vector,
        matrix,
        vector,
    )
    sizes = (mesh.shape["rep"], mesh.shape["fsdp"], mesh.shape["ctx"])
    return jax.shard_map(
        functools.partial(on_device, sizes),
        mesh=mesh,
        in_specs=(rows,) + params + (rows,),
        out_specs=(rows, rows) + params,
        check_vma=False,
    )
```
